512 devices in a mesh: mem: 8 (over x, core), space: 64 (over z, y).
Axes of the slice: x: 4, y: 4, z: 16, core: 2. Of those that a mesh axis runs over, the one named last changes fastest.
Arguments:
- ensemble: float32 [80, 8, 256, 640], P('mem', None, 'space'), may hold values from -6 to 6
- diffusivity: float32 [256, 640], P('space'), may hold values from 0.04 to 0.2
- obs_row: int32 [256], replicated, may hold values from 0 to 255
- obs_lon: int32 [256], replicated, may hold values from 0 to 639
- obs_level: int32 [256], replicated, may hold values from 0 to 7
- obs_order: int32 [256], replicated, may hold values from 0 to 255, each once
- obs_value: float32 [256], replicated, may hold values from -6 to 6
- obs_error: float32 [256], replicated, may hold values from 0.1 to 2
- coupling: float32 [8, 8], replicated, may hold values from 0.3 to 1
Outputs:
- analysis: float32 [80, 8, 256, 640], P(None, 'mem', 'space')
The draws below stay inside these ranges and needn't reach their ends.
All inputs are finite; a program needn't handle non-finite values.
Results may differ from the reference program's by a relative error of at most 0.00011.
Values sent between devices are 32-bit elements; how exact they have to be, the bound alone decides.
No kernel may reach another device: no remote copies, remote signals or barrier semaphores. Data moves between devices by JAX's collectives and lax.ppermute only.
A program may use at most 64 MiB of HBM per device.

```python
import math
import jax
import jax.numpy as jnp
import numpy as np
from jax import lax

M = 80
V = 4
L = 2
NLON = 640
OBS_BLOCK = 128
BLOCKS = 2
NLAT = 256
NOBS = 256
LOC_RADIUS = 16


def place_ends(drawn, stream_key, least, top_value):
    shape = drawn.shape
    spot = [jax.random.randint(jax.random.fold_in(stream_key, axis), (), 0, shape[axis]) for axis in range(len(shape))]
    drawn = drawn.at[tuple(spot)].set(least)
    longest = shape.index(max(shape))
    spot[longest] = (spot[longest] + 1) % shape[longest]
    return drawn.at[tuple(spot)].set(top_value)


def block_levels(own_key, shape, pieces, smallest, largest):
    def one(dim, shards_of):
        draws = jax.random.uniform(jax.random.fold_in(jax.random.fold_in(own_key, 6), dim), (shards_of,), jnp.float32, smallest / len(pieces), largest / len(pieces))
        return jnp.repeat(jnp.exp(draws), shape[dim] // shards_of).reshape((-1,) + (1,) * (len(shape) - dim - 1))

    level = one(*pieces[0])
    for cut in pieces[1:]:
        level = level * one(*cut)
    return level


def cumulative_ranks(number_of, lean):
    loads = [(1 << 20) // math.isqrt(standing ** lean) + 1 for standing in range(1, number_of + 1)]
    scale = 1 + sum(loads) // (1 << 30)
    return np.cumsum(np.array([max(1, weight // scale) for weight in loads]))


def ranked_ids(own_key, dims, count, slope):
    grid = cumulative_ranks(count, slope)
    lot = jax.random.randint(jax.random.fold_in(own_key, 1), dims, 0, int(grid[count - 1]))
    grade = jnp.searchsorted(jnp.asarray(grid, jnp.int32), lot, side="right")
    return jax.random.permutation(jax.random.fold_in(own_key, 2), count)[grade].astype(jnp.int32)


def bell_draw(key, extent, spread, bound, cuts=(), kind=jnp.bfloat16):
    entries = spread * jax.random.normal(key, extent, jnp.float32)
    if cuts:
        entries = entries * block_levels(key, extent, cuts, -0.22, 0.18)
    return jnp.clip(entries, -bound, bound).astype(kind)


def setup_inputs(seed: int = 0) -> dict:
    splits = jax.random.split(jax.random.key(seed), 10)
    return {
        "ensemble": bell_draw(splits[0], (M, V * L, NLAT, NLON), 1.0, 6.0, ((0, 8), (2, 64)), jnp.float32),
        "diffusivity": jnp.clip(jnp.exp(math.log(0.2) - 1.609438 * jax.random.uniform(splits[1], (NLAT, NLON), jnp.float32) ** block_levels(splits[1], (NLAT, NLON), ((0, 64),), -0.2, 0.2)), 0.04, 0.2),
        "obs_row": place_ends(ranked_ids(splits[2], (NOBS,), NLAT, 3), jax.random.fold_in(splits[2], 3), 0, NLAT - 1).astype(jnp.int32),
        "obs_lon": place_ends(jax.random.randint(splits[3], (NOBS,), 0, NLON), jax.random.fold_in(splits[3], 1), 0, NLON - 1).astype(jnp.int32),
        "obs_level": place_ends(jax.random.randint(splits[4], (NOBS,), 0, V * L), jax.random.fold_in(splits[4], 1), 0, (V * L) - 1).astype(jnp.int32),
        "obs_order": jax.random.permutation(splits[5], NOBS).astype(jnp.int32),
        "obs_value": bell_draw(splits[6], (NOBS,), 1.5, 6.0, (), jnp.float32),
        "obs_error": jnp.clip(jnp.exp(jax.random.uniform(splits[7], (NOBS,), jnp.float32, math.log(0.1), math.log(2.0))), 0.1, 2.0),
        "coupling": jnp.clip(jax.random.uniform(splits[8], (V * L, V * L), jnp.float32, 0.3, 1.0), 0.3, 1.0),
    }


ADVECT = 0.15

def advance(padded, diff):
    centre = padded[..., 1:-1, :]
    north = padded[..., 2:, :]
    south = padded[..., :-2, :]
    east = jnp.roll(centre, -1, axis=-1)
    west = jnp.roll(centre, 1, axis=-1)
    lead = centre.shape[:-3]
    rows = centre.shape[-2]
    width = centre.shape[-1]

    def grouped(field):
        return field.reshape(lead + (V, field.shape[-3] // V, rows, width))
    here, right, left, upper, lower = (grouped(centre), grouped(east), grouped(west), grouped(north), grouped(south))
    wind_u = here[..., 0:1, :, :, :]
    wind_w = here[..., 1:2, :, :, :]
    moved = here - ADVECT * (wind_u * (right - left) + wind_w * (upper - lower))
    moved = moved + diff * (right + left + upper + lower - 4.0 * here)
    return moved.reshape(centre.shape)

def adjust(prior, values, errors):
    members = prior.shape[0]
    mean = lax.optimization_barrier(jnp.mean(prior, axis=0))
    dev = prior - mean
    var = lax.optimization_barrier(jnp.sum(dev * dev, axis=0)) / (members - 1) + 1e-06
    post_var = 1.0 / (1.0 / var + 1.0 / errors)
    post_mean = post_var * (mean / var + values / errors)
    shrink = jnp.sqrt(errors / (errors + var))
    incr = post_mean + shrink * dev - prior
    gain = dev / ((members - 1) * var)
    return (incr, gain)

def spread_weights(cell_rows, cell_lons, rows, lons, width, radius):
    dist_rows = jnp.abs(cell_rows[None, :, None] - rows[:, None, None])
    dist_lons = jnp.abs(cell_lons[None, None, :] - lons[:, None, None])
    dist_lons = jnp.minimum(dist_lons, width - dist_lons)
    dist = (dist_rows + dist_lons).astype(jnp.float32)
    near = jnp.maximum(jnp.float32(0.0), 1.0 - dist / radius)
    return near * near

def reference(ensemble, diffusivity, obs_row, obs_lon, obs_level, obs_order, obs_value, obs_error, coupling):

    def one_member(field):
        for sub in range(2):
            padded = jnp.pad(field, ((0, 0), (1, 1), (0, 0)))
            field = advance(padded, diffusivity)
        return field
    state = lax.map(one_member, ensemble)
    levels = state.shape[1]
    for block in range(BLOCKS):
        pick = obs_order[block * OBS_BLOCK:(block + 1) * OBS_BLOCK]
        rows = obs_row[pick]
        lons = obs_lon[pick]
        levs = obs_level[pick]
        prior = state[:, levs, rows, lons]
        incr, gain = adjust(prior, obs_value[pick], obs_error[pick])
        spatial = spread_weights(jnp.arange(NLAT, dtype=jnp.int32), jnp.arange(NLON, dtype=jnp.int32), rows, lons, NLON, float(LOC_RADIUS))
        couple_table = coupling[levs]

        def update_level(j, carry):
            column = lax.dynamic_index_in_dim(carry, j, axis=1, keepdims=False)
            flat = column.reshape(M, -1)
            couple = lax.dynamic_index_in_dim(couple_table, j, axis=1, keepdims=False)
            weights = (couple[:, None, None] * spatial).reshape(OBS_BLOCK, -1)
            coef = jnp.dot(gain.T, flat, precision=lax.Precision.HIGHEST)
            delta = jnp.dot(incr, weights * coef, precision=lax.Precision.HIGHEST)
            fresh = (flat + delta).reshape(M, 1, NLAT, NLON)
            return lax.dynamic_update_slice_in_dim(carry, fresh, j, axis=1)
        state = lax.fori_loop(0, levels, update_level, state)
    return state
```

```python
import jax
import jax.numpy as jnp
from jax import lax
from jax.experimental import pallas as pl
from jax.experimental.pallas import tpu as pltpu
from jax.sharding import Mesh
from jax.sharding import PartitionSpec as P

V = 4
OBS_BLOCK = 128
LOC_RADIUS = 16
ADVECT = 0.15
HALO = 2
LANES = 128
FULL = lax.Precision.HIGHEST


def vmem_specs(count):
    return [pl.BlockSpec(memory_space=pltpu.VMEM)] * count


def params():
    return pltpu.CompilerParams(vmem_limit_bytes=48 * 1024 * 1024)


def prepare(tile_rows, width, place_ref, row_ref, lon_ref, lev_ref, order_ref, value_ref, error_ref,
            coupling_ref, fields_ref, weight_ref, cross_ref, onehot_ref, pick_ref):
    count = row_ref.shape[1]
    levels = coupling_ref.shape[0]
    tile_start = place_ref[0]
    own_level = place_ref[1]
    fields = jnp.concatenate(
        [
            row_ref[...].astype(jnp.float32),
            lon_ref[...].astype(jnp.float32),
            lev_ref[...].astype(jnp.float32),
            value_ref[...],
            error_ref[...],
            jnp.zeros((3, count), jnp.float32),
        ],
        axis=0,
    )
    source = lax.broadcasted_iota(jnp.int32, (count, count), 0)
    taken = (source == order_ref[...]).astype(jnp.float32)
    ordered = jnp.dot(fields, taken, precision=FULL, preferred_element_type=jnp.float32)
    fields_ref[...] = ordered
    rows = ordered[0:1]
    lons = ordered[1:2]
    levs = ordered[2:3]
    columns = jnp.concatenate([ordered, jnp.zeros((LANES - 8, count), jnp.float32)], axis=0).T
    row_col = columns[:, 0:1]
    lon_col = columns[:, 1:2]
    lev_col = columns[:, 2:3]

    def near(drow, dlon):
        dlon = jnp.minimum(dlon, width - dlon)
        close = jnp.maximum(0.0, 1.0 - (drow + dlon) / LOC_RADIUS)
        return close * close

    coupled = jnp.zeros((count, levels), jnp.float32)
    coupled_own = jnp.zeros((count, 1), jnp.float32)
    table = coupling_ref[...]
    lane = lax.broadcasted_iota(jnp.int32, (levels, levels), 1)
    own = jnp.sum(jnp.where(lane == own_level, table, 0.0), axis=1, keepdims=True)
    for level in range(levels):
        here = lev_col == level
        coupled = jnp.where(here, table[level:level + 1, :], coupled)
        coupled_own = jnp.where(here, own[level:level + 1, :], coupled_own)
    cell_lon = lax.broadcasted_iota(jnp.int32, (1, width), 1).astype(jnp.float32)
    dlon = jnp.abs(cell_lon - lon_col)
    for row in range(tile_rows):
        drow = jnp.abs((tile_start + row).astype(jnp.float32) - row_col)
        weight_ref[row] = coupled_own * near(drow, dlon)

    first = slice(0, OBS_BLOCK)
    second = slice(OBS_BLOCK, 2 * OBS_BLOCK)
    between = jnp.zeros((OBS_BLOCK, OBS_BLOCK), jnp.float32)
    for level in range(levels):
        between = jnp.where(levs[:, second] == level, coupled[first, level:level + 1], between)
    cross_ref[...] = between * near(
        jnp.abs(row_col[first] - rows[:, second]), jnp.abs(lon_col[first] - lons[:, second])
    )

    lon_id = lax.broadcasted_iota(jnp.int32, (width, count), 0).astype(jnp.float32)
    onehot_ref[...] = (lon_id == lons).astype(jnp.bfloat16)
    slot = lax.broadcasted_iota(jnp.int32, (8, count), 0).astype(jnp.float32)
    local = rows - tile_start.astype(jnp.float32) + HALO
    inside = (slot == local) & (slot >= HALO) & (slot < HALO + tile_rows)
    for level in range(levels):
        pick_ref[level] = jnp.where(inside & (levs == level), 1.0, 0.0)


def forecast(x_ref, low_ref, high_ref, diff_ref, onehot_ref, pick_ref, out_ref, prior_ref, wide_ref):
    members, levels, tile_rows, width = x_ref.shape
    deep = tile_rows + 2 * HALO
    heights = levels // V
    extra = members * levels
    diff = jnp.concatenate([low_ref[extra], diff_ref[...], high_ref[extra]], axis=0)

    def sub_step(fields):
        wind_u, wind_w = fields[0], fields[1]
        moved = []
        for q in fields:
            east = pltpu.roll(q, width - 1, 1)
            west = pltpu.roll(q, 1, 1)
            north = pltpu.roll(q, deep - 1, 0)
            south = pltpu.roll(q, 1, 0)
            new = q - ADVECT * (wind_u * (east - west) + wind_w * (north - south))
            moved.append(new + diff * (east + west + north + south - 4.0 * q))
        return moved

    @pl.loop(0, members)
    def _(member):
        for height in range(heights):
            fields = []
            for v in range(V):
                level = v * heights + height
                at = member * levels + level
                fields.append(
                    jnp.concatenate([low_ref[at], x_ref[member, level], high_ref[at]], axis=0)
                )
            fields = sub_step(sub_step(fields))
            for v in range(V):
                level = v * heights + height
                out_ref[level, member] = fields[v][HALO:HALO + tile_rows]
                wide_ref[level, member] = fields[v]

    def gather(level, total):
        rest = wide_ref[level].reshape(members * deep, width)
        found = jnp.zeros((members * deep, onehot_ref.shape[1]), jnp.float32)
        for _ in range(3):
            part = rest.astype(jnp.bfloat16)
            rest = rest - part.astype(jnp.float32)
            found = found + jnp.dot(part, onehot_ref[...], preferred_element_type=jnp.float32)
        return total + found.reshape(members, deep, -1) * pick_ref[level][None]

    total = lax.fori_loop(
        0, levels, gather, jnp.zeros((members, deep, onehot_ref.shape[1]), jnp.float32)
    )
    prior_ref[...] = jnp.sum(total, axis=1)


def adjust(prior, values, errors):
    members = prior.shape[0]
    mean = jnp.sum(prior, axis=0, keepdims=True) / members
    dev = prior - mean
    var = jnp.sum(dev * dev, axis=0, keepdims=True) / (members - 1) + 1e-06
    post_var = 1.0 / (1.0 / var + 1.0 / errors)
    post_mean = post_var * (mean / var + values / errors)
    shrink = jnp.sqrt(errors / (errors + var))
    incr = post_mean + shrink * dev - prior
    gain = dev / ((members - 1) * var)
    return incr, gain.T


def dot(a, b):
    return jnp.dot(a, b, precision=FULL, preferred_element_type=jnp.float32)


def analyse(x_ref, prior_ref, fields_ref, weight_ref, cross_ref, out_ref):
    members, tile_rows, _ = x_ref.shape
    planes, tiles, share, _ = prior_ref.shape
    prior = jnp.concatenate(
        [sum(prior_ref[i, t] for t in range(tiles)) for i in range(planes)], axis=0
    )
    values = fields_ref[3:4]
    errors = fields_ref[4:5]
    first = slice(0, OBS_BLOCK)
    second = slice(OBS_BLOCK, 2 * OBS_BLOCK)
    incr0, gain0 = adjust(prior[:, first], values[:, first], errors[:, first])
    later = prior[:, second]
    later = later + dot(incr0, cross_ref[...] * dot(gain0, later))
    incr1, gain1 = adjust(later, values[:, second], errors[:, second])
    for row in range(tile_rows):
        x = x_ref[:, row, :]
        x = x + dot(incr0, weight_ref[row, first, :] * dot(gain0, x))
        x = x + dot(incr1, weight_ref[row, second, :] * dot(gain1, x))
        out_ref[:, row, :] = x


def shards(ensemble, diffusivity, obs_row, obs_lon, obs_level, obs_order, obs_value, obs_error, coupling):
    members, levels, tile_rows, width = ensemble.shape
    count = obs_row.shape[0]
    space = ("z", "y")
    mem = ("x", "core")
    tiles = lax.axis_size(space)
    planes = lax.axis_size("z")
    own_level = lax.axis_index(mem)
    place = jnp.stack([lax.axis_index(space) * tile_rows, own_level]).astype(jnp.int32)

    flat = ensemble.reshape(members * levels, tile_rows, width)
    edges = jnp.concatenate([flat, diffusivity[None]], axis=0)
    low = lax.ppermute(edges[:, tile_rows - HALO:], space, [(i, i + 1) for i in range(tiles - 1)])
    high = lax.ppermute(edges[:, :HALO], space, [(i + 1, i) for i in range(tiles - 1)])

    line = lambda a: a.reshape(1, count)
    fields, weight, cross, onehot, pick = pl.pallas_call(
        lambda *refs: prepare(tile_rows, width, *refs),
        out_shape=[
            jax.ShapeDtypeStruct((8, count), jnp.float32),
            jax.ShapeDtypeStruct((tile_rows, count, width), jnp.float32),
            jax.ShapeDtypeStruct((OBS_BLOCK, OBS_BLOCK), jnp.float32),
            jax.ShapeDtypeStruct((width, count), jnp.bfloat16),
            jax.ShapeDtypeStruct((levels, 8, count), jnp.float32),
        ],
        in_specs=[pl.BlockSpec(memory_space=pltpu.SMEM)] + vmem_specs(7),
        out_specs=vmem_specs(5),
        compiler_params=params(),
        cost_estimate=pl.CostEstimate(flops=10_000_000, bytes_accessed=4_000_000, transcendentals=0),
        name="prepare",
    )(place, line(obs_row), line(obs_lon), line(obs_level), line(obs_order), line(obs_value),
      line(obs_error), coupling)

    state, prior = pl.pallas_call(
        forecast,
        out_shape=[
            jax.ShapeDtypeStruct((levels, members, tile_rows, width), jnp.float32),
            jax.ShapeDtypeStruct((members, count), jnp.float32),
        ],
        in_specs=vmem_specs(6),
        out_specs=vmem_specs(2),
        scratch_shapes=[pltpu.VMEM((levels, members, tile_rows + 2 * HALO, width), jnp.float32)],
        compiler_params=params(),
        name="forecast",
    )(ensemble, low, high, diffusivity, onehot, pick)

    reach = 2 * (LOC_RADIUS - 1)
    tiles_reached = -(-reach // tile_rows)
    rows_of_tiles = tiles // planes
    planes_reached = min(-(-tiles_reached // rows_of_tiles), planes - 1)
    near = prior
    for d in range(1, planes_reached + 1):
        near = near + lax.ppermute(prior, "z", [(i, i + d) for i in range(planes - d)])
        near = near + lax.ppermute(prior, "z", [(i + d, i) for i in range(planes - d)])
    group = mem + ("y",)
    size = lax.axis_size(group)
    spread = lax.all_to_all(
        jnp.broadcast_to(near[None], (size, members, count)), group, 0, 0, tiled=True
    )
    spread = spread.reshape(size // rows_of_tiles, rows_of_tiles, members, count)

    state = lax.all_to_all(state, mem, 0, 0, tiled=True)
    state = state.reshape(-1, tile_rows, width)

    out = pl.pallas_call(
        analyse,
        out_shape=jax.ShapeDtypeStruct(state.shape, jnp.float32),
        in_specs=vmem_specs(5),
        out_specs=pl.BlockSpec(memory_space=pltpu.VMEM),
        compiler_params=params(),
        name="analyse",
    )(state, spread, fields, weight, cross)
    return out[:, None]


def solution(mesh):
    y = 4
    x = mesh.shape["mem"] // 2
    fine = Mesh(
        mesh.devices.reshape(x, 2, mesh.shape["space"] // y, y), ("x", "core", "z", "y")
    )
    mem, space = ("x", "core"), ("z", "y")
    placed = (P(mem, None, space, None), P(space, None), P(), P(), P(), P(), P(), P(), P())
    return jax.shard_map(
        shards, mesh=fine, in_specs=placed, out_specs=P(None, mem, space, None), check_vma=False
    )
```

```python
import jax
import jax.numpy as jnp
from jax import lax
from jax.experimental import pallas as pl
from jax.experimental.pallas import tpu as pltpu
from jax.sharding import Mesh
from jax.sharding import PartitionSpec as P

V = 4
OBS_BLOCK = 128
LOC_RADIUS = 16
ADVECT = 0.15
HALO = 2
LANES = 128
FULL = lax.Precision.HIGHEST


def vmem_specs(count):
    return [pl.BlockSpec(memory_space=pltpu.VMEM)] * count


def hbm_specs(count):
    return [pl.BlockSpec(memory_space=pltpu.HBM)] * count


def in_hbm(*arrays):
    return [pltpu.with_memory_space_constraint(a, pltpu.HBM) for a in arrays]


def fetch(pairs, sems):
    copies = [pltpu.make_async_copy(a, b, sems.at[i]) for i, (a, b) in enumerate(pairs)]
    for copy in copies:
        copy.start()
    for copy in copies:
        copy.wait()


def params(mib):
    return pltpu.CompilerParams(vmem_limit_bytes=mib * 1024 * 1024)


def prepare(tile_rows, width, place_ref, row_hbm, lon_hbm, lev_hbm, order_hbm, value_hbm, error_hbm,
            coupling_hbm, fields_ref, weight_ref, cross_ref, onehot_ref, pick_ref,
            ints, floats, coupling_ref, sems):
    count = row_hbm.shape[1]
    fetch(
        [(ref, ints.at[i]) for i, ref in enumerate((row_hbm, lon_hbm, lev_hbm, order_hbm))]
        + [(ref, floats.at[i]) for i, ref in enumerate((value_hbm, error_hbm))]
        + [(coupling_hbm, coupling_ref)],
        sems,
    )
    levels = coupling_ref.shape[0]
    tile_start = place_ref[0]
    own_level = place_ref[1]
    fields = jnp.concatenate(
        [
            ints[0].astype(jnp.float32),
            ints[1].astype(jnp.float32),
            ints[2].astype(jnp.float32),
            floats[0],
            floats[1],
            jnp.zeros((3, count), jnp.float32),
        ],
        axis=0,
    )
    source = lax.broadcasted_iota(jnp.int32, (count, count), 0)
    taken = (source == ints[3]).astype(jnp.float32)
    ordered = jnp.dot(fields, taken, precision=FULL, preferred_element_type=jnp.float32)
    fields_ref[...] = ordered
    rows = ordered[0:1]
    lons = ordered[1:2]
    levs = ordered[2:3]
    columns = jnp.concatenate([ordered, jnp.zeros((LANES - 8, count), jnp.float32)], axis=0).T
    row_col = columns[:, 0:1]
    lon_col = columns[:, 1:2]
    lev_col = columns[:, 2:3]

    def near(drow, dlon):
        dlon = jnp.minimum(dlon, width - dlon)
        close = jnp.maximum(0.0, 1.0 - (drow + dlon) / LOC_RADIUS)
        return close * close

    coupled = jnp.zeros((count, levels), jnp.float32)
    coupled_own = jnp.zeros((count, 1), jnp.float32)
    table = coupling_ref[...]
    lane = lax.broadcasted_iota(jnp.int32, (levels, levels), 1)
    own = jnp.sum(jnp.where(lane == own_level, table, 0.0), axis=1, keepdims=True)
    for level in range(levels):
        here = lev_col == level
        coupled = jnp.where(here, table[level:level + 1, :], coupled)
        coupled_own = jnp.where(here, own[level:level + 1, :], coupled_own)
    cell_lon = lax.broadcasted_iota(jnp.int32, (1, width), 1).astype(jnp.float32)
    dlon = jnp.abs(cell_lon - lon_col)
    for row in range(tile_rows):
        drow = jnp.abs((tile_start + row).astype(jnp.float32) - row_col)
        weight_ref[:, row * width:(row + 1) * width] = coupled_own * near(drow, dlon)

    first = slice(0, OBS_BLOCK)
    second = slice(OBS_BLOCK, 2 * OBS_BLOCK)
    between = jnp.zeros((OBS_BLOCK, OBS_BLOCK), jnp.float32)
    for level in range(levels):
        between = jnp.where(levs[:, second] == level, coupled[first, level:level + 1], between)
    cross_ref[...] = between * near(
        jnp.abs(row_col[first] - rows[:, second]), jnp.abs(lon_col[first] - lons[:, second])
    )

    lon_id = lax.broadcasted_iota(jnp.int32, (width, count), 0).astype(jnp.float32)
    onehot_ref[...] = (lon_id == lons).astype(jnp.bfloat16)
    heights = levels // V
    slot = lax.broadcasted_iota(jnp.int32, (8, count), 0)
    height = slot // tile_rows
    inside = rows - tile_start.astype(jnp.float32) == (slot - height * tile_rows).astype(jnp.float32)
    for v in range(V):
        there = levs == (v * heights + height).astype(jnp.float32)
        pick_ref[v] = jnp.where(inside & there, 1.0, 0.0)


def edges(x_hbm, diff_hbm, up_ref, down_ref, held_ref, diff_ref, sems):
    tile_rows = x_hbm.shape[1]
    extra = x_hbm.shape[0]
    fetch([(x_hbm, held_ref), (diff_hbm, diff_ref)], sems)
    up_ref[0:extra] = held_ref[:, tile_rows - HALO:, :]
    down_ref[0:extra] = held_ref[:, :HALO, :]
    up_ref[extra] = diff_ref[tile_rows - HALO:, :]
    down_ref[extra] = diff_ref[:HALO, :]


def forecast(x_hbm, diff_hbm, low_hbm, high_hbm, onehot_ref, pick_ref, prior_ref, out_hbm,
             wide_ref, own_ref, pair_ref, diff_ref, diff_sems, in_sems, out_sems):
    members, levels, tile_rows, width = x_hbm.shape
    heights = levels // V
    deep = tile_rows + 2 * HALO
    extra = members * levels
    top, own, bottom = pl.ds(0, HALO), pl.ds(HALO, tile_rows), pl.ds(HALO + tile_rows, HALO)

    def arrivals(member):
        part = pl.ds(member * levels, levels)
        return [
            pltpu.make_async_copy(x_hbm.at[member], wide_ref.at[member, :, own], in_sems.at[member, 0]),
            pltpu.make_async_copy(low_hbm.at[part], wide_ref.at[member, :, top], in_sems.at[member, 1]),
            pltpu.make_async_copy(high_hbm.at[part], wide_ref.at[member, :, bottom], in_sems.at[member, 2]),
        ]

    def departure(member):
        return pltpu.make_async_copy(own_ref.at[:, member], out_hbm.at[:, member], out_sems.at[member])

    diffs = [
        pltpu.make_async_copy(diff_hbm, diff_ref.at[own], diff_sems.at[0]),
        pltpu.make_async_copy(low_hbm.at[extra], diff_ref.at[top], diff_sems.at[1]),
        pltpu.make_async_copy(high_hbm.at[extra], diff_ref.at[bottom], diff_sems.at[2]),
    ]
    for copy in diffs:
        copy.start()
    for member in range(members):
        for copy in arrivals(member):
            copy.start()
    for copy in diffs:
        copy.wait()
    diff = diff_ref[...]
    keep = 1.0 - 4.0 * diff
    upper = lax.broadcasted_iota(jnp.int32, (deep, width), 0) < tile_rows

    def sub_step(fields):
        push_u, push_w = ADVECT * fields[0], ADVECT * fields[1]
        from_east, from_west = diff - push_u, diff + push_u
        from_north, from_south = diff - push_w, diff + push_w
        return [
            keep * q
            + (from_east * pltpu.roll(q, width - 1, 1) + from_west * pltpu.roll(q, 1, 1))
            + (from_north * pltpu.roll(q, deep - 1, 0) + from_south * pltpu.roll(q, 1, 0))
            for q in fields
        ]

    @pl.loop(0, members)
    def _(member):
        for copy in arrivals(member):
            copy.wait()
        done = []
        for height in range(heights):
            fields = sub_step(sub_step([wide_ref[member, v * heights + height] for v in range(V)]))
            for v in range(V):
                own_ref[v * heights + height, member] = fields[v][HALO:HALO + tile_rows]
            done.append(fields)
        departure(member).start()
        for v in range(V):
            pair_ref[v, member] = jnp.where(
                upper, pltpu.roll(done[0][v], deep - HALO, 0), pltpu.roll(done[1][v], HALO, 0)
            )

    count = onehot_ref.shape[1]
    total = jnp.zeros((members, deep, count), jnp.float32)
    for v in range(V):
        rest = pair_ref[v].reshape(members * deep, width)
        found = jnp.zeros((members * deep, count), jnp.float32)
        for _ in range(3):
            part = rest.astype(jnp.bfloat16)
            rest = rest - part.astype(jnp.float32)
            found = found + jnp.dot(part, onehot_ref[...], preferred_element_type=jnp.float32)
        total = total + found.reshape(members, deep, -1) * pick_ref[v][None]
    prior = jnp.sum(total, axis=1)
    for m in range(members):
        prior_ref[:, m * count:(m + 1) * count] = prior[m:m + 1]
    for member in range(members):
        departure(member).wait()


def split(a):
    high = a.astype(jnp.bfloat16)
    return high, (a - high.astype(jnp.float32)).astype(jnp.bfloat16)

def exactdot(a, b):
    return jnp.dot(a, b, precision=lax.Precision.HIGHEST, preferred_element_type=jnp.float32)

def adjust(prior, values, errors):
    members = prior.shape[0]
    mean = jnp.sum(prior, axis=0, keepdims=True) / members
    dev = prior - mean
    var = jnp.sum(dev * dev, axis=0, keepdims=True) / (members - 1) + 1e-06
    post_var = 1.0 / (1.0 / var + 1.0 / errors)
    post_mean = post_var * (mean / var + values / errors)
    shrink = jnp.sqrt(errors / (errors + var))
    incr = post_mean + shrink * dev - prior
    gain = dev / ((members - 1) * var)
    return incr, gain

def three(a, axis):
    high, low = split(a)
    order = [high, high, low] if axis == 1 else [high, low, high]
    return jnp.concatenate(order, axis=axis)

def thin(gain):
    high = gain.astype(jnp.bfloat16).astype(jnp.float32)
    return jnp.concatenate([high, high, gain - high], axis=0).T.astype(jnp.bfloat16)

def onedot(a, b):
    return jnp.dot(a, b, preferred_element_type=jnp.float32)

def analyse(x_ref, prior_ref, fields_ref, weight_ref, cross_ref, out_ref, scratch):
    members, tile_rows, width = x_ref.shape
    planes, tiles, _, _ = prior_ref.shape
    count = fields_ref.shape[1]
    share = members // planes
    for i in range(planes):
        for m in range(share):
            at = slice(m * count, (m + 1) * count)
            line = prior_ref[i, 0, :, at]
            for t in range(1, tiles):
                line = line + prior_ref[i, t, :, at]
            scratch[i * share + m:i * share + m + 1, :] = line
    prior = scratch[...]
    values = fields_ref[3:4]
    errors = fields_ref[4:5]
    first = slice(0, OBS_BLOCK)
    second = slice(OBS_BLOCK, 2 * OBS_BLOCK)
    incr0, gain0 = adjust(prior[:, first], values[:, first], errors[:, first])
    later = prior[:, second]
    later = later + exactdot(incr0, cross_ref[...] * exactdot(gain0.T, later))
    incr1, gain1 = adjust(later, values[:, second], errors[:, second])
    incr0, incr1 = three(incr0, 1), three(incr1, 1)
    gain0, gain1 = thin(gain0), thin(gain1)
    x = jnp.concatenate([x_ref[:, row, :] for row in range(tile_rows)], axis=1)
    x = x + onedot(incr0, three(weight_ref[first, :] * onedot(gain0, three(x, 0)), 0))
    x = x + onedot(incr1, three(weight_ref[second, :] * onedot(gain1, three(x, 0)), 0))
    for row in range(tile_rows):
        out_ref[:, row, :] = x[:, row * width:(row + 1) * width]


def shards(ensemble, diffusivity, obs_row, obs_lon, obs_level, obs_order, obs_value, obs_error, coupling):
    members, levels, tile_rows, width = ensemble.shape
    count = obs_row.shape[0]
    space = ("z", "y")
    mem = ("x", "core")
    tiles = lax.axis_size(space)
    planes = lax.axis_size("z")
    own_level = lax.axis_index(mem)
    place = jnp.stack([lax.axis_index(space) * tile_rows, own_level]).astype(jnp.int32)
    cells = tile_rows * width
    shape = jax.ShapeDtypeStruct
    f32 = jnp.float32

    extra = members * levels
    flat = ensemble.reshape(extra, tile_rows, width)
    up, down = pl.pallas_call(
        edges,
        out_shape=[
            shape((extra + 1, HALO, width), f32),
            shape((extra + 1, HALO, width), f32),
        ],
        in_specs=hbm_specs(2),
        out_specs=vmem_specs(2),
        scratch_shapes=[
            pltpu.VMEM((extra, tile_rows, width), f32),
            pltpu.VMEM((tile_rows, width), f32),
            pltpu.SemaphoreType.DMA((2,)),
        ],
        compiler_params=params(8),
        name="edges",
    )(*in_hbm(flat, diffusivity))
    low = lax.ppermute(up, space, [(i, i + 1) for i in range(tiles - 1)])
    high = lax.ppermute(down, space, [(i + 1, i) for i in range(tiles - 1)])

    line = lambda a: a.reshape(1, count)
    fields, weight, cross, onehot, pick = pl.pallas_call(
        lambda *refs: prepare(tile_rows, width, *refs),
        out_shape=[
            shape((8, count), f32),
            shape((count, cells), f32),
            shape((OBS_BLOCK, OBS_BLOCK), f32),
            shape((width, count), jnp.bfloat16),
            shape((V, 8, count), f32),
        ],
        in_specs=[pl.BlockSpec(memory_space=pltpu.SMEM)] + hbm_specs(7),
        out_specs=vmem_specs(5),
        scratch_shapes=[
            pltpu.VMEM((4, 1, count), jnp.int32),
            pltpu.VMEM((2, 1, count), f32),
            pltpu.VMEM((levels, levels), f32),
            pltpu.SemaphoreType.DMA((7,)),
        ],
        compiler_params=params(16),
        cost_estimate=pl.CostEstimate(flops=10_000_000, bytes_accessed=4_000_000, transcendentals=0),
        name="prepare",
    )(place, *in_hbm(line(obs_row), line(obs_lon), line(obs_level), line(obs_order), line(obs_value),
                     line(obs_error), coupling))

    deep = tile_rows + 2 * HALO
    prior, state = pl.pallas_call(
        forecast,
        out_shape=[
            shape((1, members * count), f32),
            pltpu.HBM((levels, members, tile_rows, width), f32),
        ],
        in_specs=hbm_specs(4) + vmem_specs(2),
        out_specs=vmem_specs(1) + hbm_specs(1),
        scratch_shapes=[
            pltpu.VMEM((members, levels, deep, width), f32),
            pltpu.VMEM((levels, members, tile_rows, width), f32),
            pltpu.VMEM((V, members, deep, width), f32),
            pltpu.VMEM((deep, width), f32),
            pltpu.SemaphoreType.DMA((3,)),
            pltpu.SemaphoreType.DMA((members, 3)),
            pltpu.SemaphoreType.DMA((members,)),
        ],
        compiler_params=params(16),
        name="forecast",
    )(*in_hbm(ensemble, diffusivity), low, high, onehot, pick)

    reach = 2 * (LOC_RADIUS - 1)
    tiles_reached = -(-reach // tile_rows)
    rows_of_tiles = tiles // planes
    planes_reached = min(-(-tiles_reached // rows_of_tiles), planes - 1)
    near = prior
    for d in range(1, planes_reached + 1):
        near = near + lax.ppermute(prior, "z", [(i, i + d) for i in range(planes - d)])
        near = near + lax.ppermute(prior, "z", [(i + d, i) for i in range(planes - d)])
    state = lax.all_to_all(state, mem, 0, 0, tiled=True)
    near, state = lax.optimization_barrier((near, state))
    group = mem + ("y",)
    size = lax.axis_size(group)
    spread = lax.all_to_all(
        jnp.broadcast_to(near[None], (size,) + near.shape), group, 0, 0, tiled=True
    )
    spread = spread.reshape((size // rows_of_tiles, rows_of_tiles) + near.shape)
    state = state.reshape(-1, tile_rows, width)

    out = pl.pallas_call(
        analyse,
        out_shape=shape(state.shape, f32),
        in_specs=vmem_specs(5),
        out_specs=pl.BlockSpec(memory_space=pltpu.VMEM),
        scratch_shapes=[pltpu.VMEM((state.shape[0], count), f32)],
        compiler_params=params(24),
        name="analyse",
    )(state, spread, fields, weight, cross)
    return out[:, None]


def solution(mesh):
    y = 4
    x = mesh.shape["mem"] // 2
    fine = Mesh(
        mesh.devices.reshape(x, 2, mesh.shape["space"] // y, y), ("x", "core", "z", "y")
    )
    mem, space = ("x", "core"), ("z", "y")
    placed = (P(mem, None, space, None), P(space, None), P(), P(), P(), P(), P(), P(), P())
    return jax.shard_map(
        shards, mesh=fine, in_specs=placed, out_specs=P(None, mem, space, None), check_vma=False
    )
```

```python
import jax
import jax.numpy as jnp
from jax import lax
from jax.experimental import pallas as pl
from jax.experimental.pallas import tpu as pltpu
from jax.sharding import Mesh
from jax.sharding import PartitionSpec as P

V = 4
OBS_BLOCK = 128
LOC_RADIUS = 16
ADVECT = 0.15
HALO = 2
LANES = 128
FULL = lax.Precision.HIGHEST


def vmem_specs(count):
    return [pl.BlockSpec(memory_space=pltpu.VMEM)] * count


def hbm_specs(count):
    return [pl.BlockSpec(memory_space=pltpu.HBM)] * count


def in_hbm(*arrays):
    return [pltpu.with_memory_space_constraint(a, pltpu.HBM) for a in arrays]


def fetch(pairs, sems):
    copies = [pltpu.make_async_copy(a, b, sems.at[i]) for i, (a, b) in enumerate(pairs)]
    for copy in copies:
        copy.start()
    for copy in copies:
        copy.wait()


def params(mib):
    return pltpu.CompilerParams(vmem_limit_bytes=mib * 1024 * 1024)


def prepare(tile_rows, width, place_ref, row_hbm, lon_hbm, lev_hbm, order_hbm, value_hbm, error_hbm,
            coupling_hbm, fields_ref, weight_ref, cross_ref, onehot_ref, pick_ref,
            ints, floats, coupling_ref, sems):
    count = row_hbm.shape[1]
    fetch(
        [(ref, ints.at[i]) for i, ref in enumerate((row_hbm, lon_hbm, lev_hbm, order_hbm))]
        + [(ref, floats.at[i]) for i, ref in enumerate((value_hbm, error_hbm))]
        + [(coupling_hbm, coupling_ref)],
        sems,
    )
    levels = coupling_ref.shape[0]
    tile_start = place_ref[0]
    own_level = place_ref[1]
    fields = jnp.concatenate(
        [
            ints[0].astype(jnp.float32),
            ints[1].astype(jnp.float32),
            ints[2].astype(jnp.float32),
            floats[0],
            floats[1],
            jnp.zeros((3, count), jnp.float32),
        ],
        axis=0,
    )
    source = lax.broadcasted_iota(jnp.int32, (count, count), 0)
    taken = (source == ints[3]).astype(jnp.float32)
    ordered = jnp.dot(fields, taken, precision=FULL, preferred_element_type=jnp.float32)
    fields_ref[...] = ordered
    rows = ordered[0:1]
    lons = ordered[1:2]
    levs = ordered[2:3]
    columns = jnp.concatenate([ordered, jnp.zeros((LANES - 8, count), jnp.float32)], axis=0).T
    row_col = columns[:, 0:1]
    lon_col = columns[:, 1:2]
    lev_col = columns[:, 2:3]

    def near(drow, dlon):
        dlon = jnp.minimum(dlon, width - dlon)
        close = jnp.maximum(0.0, 1.0 - (drow + dlon) / LOC_RADIUS)
        return close * close

    coupled = jnp.zeros((count, levels), jnp.float32)
    coupled_own = jnp.zeros((count, 1), jnp.float32)
    table = coupling_ref[...]
    lane = lax.broadcasted_iota(jnp.int32, (levels, levels), 1)
    own = jnp.sum(jnp.where(lane == own_level, table, 0.0), axis=1, keepdims=True)
    for level in range(levels):
        here = lev_col == level
        coupled = jnp.where(here, table[level:level + 1, :], coupled)
        coupled_own = jnp.where(here, own[level:level + 1, :], coupled_own)
    cell_lon = lax.broadcasted_iota(jnp.int32, (1, width), 1).astype(jnp.float32)
    dlon = jnp.abs(cell_lon - lon_col)
    for row in range(tile_rows):
        drow = jnp.abs((tile_start + row).astype(jnp.float32) - row_col)
        weight_ref[:, row * width:(row + 1) * width] = coupled_own * near(drow, dlon)

    first = slice(0, OBS_BLOCK)
    second = slice(OBS_BLOCK, 2 * OBS_BLOCK)
    between = jnp.zeros((OBS_BLOCK, OBS_BLOCK), jnp.float32)
    for level in range(levels):
        between = jnp.where(levs[:, second] == level, coupled[first, level:level + 1], between)
    cross_ref[...] = between * near(
        jnp.abs(row_col[first] - rows[:, second]), jnp.abs(lon_col[first] - lons[:, second])
    )

    lon_id = lax.broadcasted_iota(jnp.int32, (width, count), 0).astype(jnp.float32)
    onehot_ref[...] = (lon_id == lons).astype(jnp.bfloat16)
    heights = levels // V
    slot = lax.broadcasted_iota(jnp.int32, (8, count), 0)
    height = slot // tile_rows
    inside = rows - tile_start.astype(jnp.float32) == (slot - height * tile_rows).astype(jnp.float32)
    for v in range(V):
        there = levs == (v * heights + height).astype(jnp.float32)
        pick_ref[v] = jnp.where(inside & there, 1.0, 0.0)


def edges(place_ref, x_hbm, diff_hbm, first_ref, second_ref, held_ref, diff_ref, sems):
    members, levels, tile_rows, width = x_hbm.shape
    extra = members * levels
    odd = place_ref[2] == 1
    copies = [pltpu.make_async_copy(diff_hbm, diff_ref, sems.at[members])]
    copies += [pltpu.make_async_copy(x_hbm.at[i], held_ref.at[i], sems.at[i]) for i in range(members)]
    for copy in copies:
        copy.start()

    def give(low_ref, high_ref):
        for member in range(members):
            part = slice(member * levels, (member + 1) * levels)
            copies[member + 1].wait()
            low_ref[part] = held_ref[member, :, :HALO, :]
            high_ref[part] = held_ref[member, :, tile_rows - HALO:, :]
        copies[0].wait()
        low_ref[extra] = diff_ref[:HALO, :]
        high_ref[extra] = diff_ref[tile_rows - HALO:, :]

    @pl.when(odd)
    def _():
        give(second_ref, first_ref)

    @pl.when(jnp.logical_not(odd))
    def _():
        give(first_ref, second_ref)


def forecast(place_ref, x_hbm, diff_hbm, first_hbm, second_hbm, onehot_ref, pick_ref, prior_ref, out_hbm,
             wide_ref, own_ref, pair_ref, diff_ref, diff_sems, in_sems, out_sems):
    members, levels, tile_rows, width = x_hbm.shape
    heights = levels // V
    deep = tile_rows + 2 * HALO
    extra = members * levels
    top, own, bottom = pl.ds(0, HALO), pl.ds(HALO, tile_rows), pl.ds(HALO + tile_rows, HALO)

    odd = place_ref[2] == 1

    def arrivals(member, low_hbm, high_hbm):
        part = pl.ds(member * levels, levels)
        return [
            pltpu.make_async_copy(x_hbm.at[member], wide_ref.at[member, :, own], in_sems.at[member, 0]),
            pltpu.make_async_copy(low_hbm.at[part], wide_ref.at[member, :, top], in_sems.at[member, 1]),
            pltpu.make_async_copy(high_hbm.at[part], wide_ref.at[member, :, bottom], in_sems.at[member, 2]),
        ]

    def departure(member):
        return pltpu.make_async_copy(own_ref.at[:, member], out_hbm.at[:, member], out_sems.at[member])

    def take(low_hbm, high_hbm):
        diffs = [
            pltpu.make_async_copy(diff_hbm, diff_ref.at[own], diff_sems.at[0]),
            pltpu.make_async_copy(low_hbm.at[extra], diff_ref.at[top], diff_sems.at[1]),
            pltpu.make_async_copy(high_hbm.at[extra], diff_ref.at[bottom], diff_sems.at[2]),
        ]
        for copy in diffs:
            copy.start()
        for member in range(members):
            for copy in arrivals(member, low_hbm, high_hbm):
                copy.start()
        for copy in diffs:
            copy.wait()

    @pl.when(odd)
    def _():
        take(second_hbm, first_hbm)

    @pl.when(jnp.logical_not(odd))
    def _():
        take(first_hbm, second_hbm)

    diff = diff_ref[...]
    keep = 1.0 - 4.0 * diff
    upper = lax.broadcasted_iota(jnp.int32, (deep, width), 0) < tile_rows

    def sub_step(fields):
        push_u, push_w = ADVECT * fields[0], ADVECT * fields[1]
        from_east, from_west = diff - push_u, diff + push_u
        from_north, from_south = diff - push_w, diff + push_w
        return [
            keep * q
            + (from_east * pltpu.roll(q, width - 1, 1) + from_west * pltpu.roll(q, 1, 1))
            + (from_north * pltpu.roll(q, deep - 1, 0) + from_south * pltpu.roll(q, 1, 0))
            for q in fields
        ]

    @pl.loop(0, members)
    def _(member):
        for copy in arrivals(member, first_hbm, second_hbm):
            copy.wait()
        done = []
        for height in range(heights):
            fields = sub_step(sub_step([wide_ref[member, v * heights + height] for v in range(V)]))
            for v in range(V):
                own_ref[v * heights + height, member] = fields[v][HALO:HALO + tile_rows]
            done.append(fields)
        departure(member).start()
        for v in range(V):
            pair_ref[v, member] = jnp.where(
                upper, pltpu.roll(done[0][v], deep - HALO, 0), pltpu.roll(done[1][v], HALO, 0)
            )

    count = onehot_ref.shape[1]
    total = jnp.zeros((members, deep, count), jnp.float32)
    for v in range(V):
        rest = pair_ref[v].reshape(members * deep, width)
        found = jnp.zeros((members * deep, count), jnp.float32)
        for _ in range(3):
            part = rest.astype(jnp.bfloat16)
            rest = rest - part.astype(jnp.float32)
            found = found + jnp.dot(part, onehot_ref[...], preferred_element_type=jnp.float32)
        total = total + found.reshape(members, deep, -1) * pick_ref[v][None]
    prior = jnp.sum(total, axis=1)
    for m in range(members):
        prior_ref[:, m * count:(m + 1) * count] = prior[m:m + 1]
    for member in range(members):
        departure(member).wait()


def split(a):
    high = a.astype(jnp.bfloat16)
    return high, (a - high.astype(jnp.float32)).astype(jnp.bfloat16)

def exactdot(a, b):
    return jnp.dot(a, b, precision=lax.Precision.HIGHEST, preferred_element_type=jnp.float32)

def adjust(prior, values, errors):
    members = prior.shape[0]
    mean = jnp.sum(prior, axis=0, keepdims=True) / members
    dev = prior - mean
    var = jnp.sum(dev * dev, axis=0, keepdims=True) / (members - 1) + 1e-06
    post_var = 1.0 / (1.0 / var + 1.0 / errors)
    post_mean = post_var * (mean / var + values / errors)
    shrink = jnp.sqrt(errors / (errors + var))
    incr = post_mean + shrink * dev - prior
    gain = dev / ((members - 1) * var)
    return incr, gain

def three(a, axis):
    high, low = split(a)
    order = [high, high, low] if axis == 1 else [high, low, high]
    return jnp.concatenate(order, axis=axis)

def thin(gain):
    high = gain.astype(jnp.bfloat16).astype(jnp.float32)
    return jnp.concatenate([high, high, gain - high], axis=0).T.astype(jnp.bfloat16)

def onedot(a, b):
    return jnp.dot(a, b, preferred_element_type=jnp.float32)

def analyse(x_ref, prior_ref, fields_ref, weight_ref, cross_ref, out_ref, scratch):
    members, tile_rows, width = x_ref.shape
    planes, tiles, _, _ = prior_ref.shape
    count = fields_ref.shape[1]
    share = members // planes
    for i in range(planes):
        for m in range(share):
            at = slice(m * count, (m + 1) * count)
            line = prior_ref[i, 0, :, at]
            for t in range(1, tiles):
                line = line + prior_ref[i, t, :, at]
            scratch[i * share + m:i * share + m + 1, :] = line
    prior = scratch[...]
    values = fields_ref[3:4]
    errors = fields_ref[4:5]
    first = slice(0, OBS_BLOCK)
    second = slice(OBS_BLOCK, 2 * OBS_BLOCK)
    incr0, gain0 = adjust(prior[:, first], values[:, first], errors[:, first])
    later = prior[:, second]
    later = later + exactdot(incr0, cross_ref[...] * exactdot(gain0.T, later))
    incr1, gain1 = adjust(later, values[:, second], errors[:, second])
    incr0, incr1 = three(incr0, 1), three(incr1, 1)
    gain0, gain1 = thin(gain0), thin(gain1)
    x = jnp.concatenate([x_ref[:, row, :] for row in range(tile_rows)], axis=1)
    x = x + onedot(incr0, three(weight_ref[first, :] * onedot(gain0, three(x, 0)), 0))
    x = x + onedot(incr1, three(weight_ref[second, :] * onedot(gain1, three(x, 0)), 0))
    for row in range(tile_rows):
        out_ref[:, row, :] = x[:, row * width:(row + 1) * width]


def shards(ensemble, diffusivity, obs_row, obs_lon, obs_level, obs_order, obs_value, obs_error, coupling):
    members, levels, tile_rows, width = ensemble.shape
    count = obs_row.shape[0]
    space = ("z", "y")
    mem = ("x", "core")
    tiles = lax.axis_size(space)
    planes = lax.axis_size("z")
    own_level = lax.axis_index(mem)
    tile = lax.axis_index(space)
    place = jnp.stack([tile * tile_rows, own_level, tile % 2]).astype(jnp.int32)
    cells = tile_rows * width
    shape = jax.ShapeDtypeStruct
    f32 = jnp.float32

    extra = members * levels
    smem = [pl.BlockSpec(memory_space=pltpu.SMEM)]
    first, second = pl.pallas_call(
        edges,
        out_shape=[pltpu.VMEM((extra + 1, HALO, width), f32)] * 2,
        in_specs=smem + hbm_specs(2),
        out_specs=vmem_specs(2),
        scratch_shapes=[
            pltpu.VMEM(ensemble.shape, f32),
            pltpu.VMEM((tile_rows, width), f32),
            pltpu.SemaphoreType.DMA((members + 1,)),
        ],
        compiler_params=params(8),
        name="edges",
    )(place, *in_hbm(ensemble, diffusivity))

    def swap(message, start):
        pairs = [(i, i + 1) for i in range(start, tiles - 1, 2)]
        return lax.ppermute(message, space, pairs + [(j, i) for i, j in pairs])

    first, second = swap(first, 1), swap(second, 0)

    line = lambda a: a.reshape(1, count)
    fields, weight, cross, onehot, pick = pl.pallas_call(
        lambda *refs: prepare(tile_rows, width, *refs),
        out_shape=[
            shape((8, count), f32),
            shape((count, cells), f32),
            shape((OBS_BLOCK, OBS_BLOCK), f32),
            shape((width, count), jnp.bfloat16),
            shape((V, 8, count), f32),
        ],
        in_specs=smem + hbm_specs(7),
        out_specs=vmem_specs(5),
        scratch_shapes=[
            pltpu.VMEM((4, 1, count), jnp.int32),
            pltpu.VMEM((2, 1, count), f32),
            pltpu.VMEM((levels, levels), f32),
            pltpu.SemaphoreType.DMA((7,)),
        ],
        compiler_params=params(16),
        cost_estimate=pl.CostEstimate(flops=10_000_000, bytes_accessed=4_000_000, transcendentals=0),
        name="prepare",
    )(place, *in_hbm(line(obs_row), line(obs_lon), line(obs_level), line(obs_order), line(obs_value),
                     line(obs_error), coupling))

    deep = tile_rows + 2 * HALO
    prior, state = pl.pallas_call(
        forecast,
        out_shape=[
            shape((1, members * count), f32),
            pltpu.HBM((levels, members, tile_rows, width), f32),
        ],
        in_specs=smem + hbm_specs(4) + vmem_specs(2),
        out_specs=vmem_specs(1) + hbm_specs(1),
        scratch_shapes=[
            pltpu.VMEM((members, levels, deep, width), f32),
            pltpu.VMEM((levels, members, tile_rows, width), f32),
            pltpu.VMEM((V, members, deep, width), f32),
            pltpu.VMEM((deep, width), f32),
            pltpu.SemaphoreType.DMA((3,)),
            pltpu.SemaphoreType.DMA((members, 3)),
            pltpu.SemaphoreType.DMA((members,)),
        ],
        compiler_params=params(16),
        name="forecast",
    )(place, *in_hbm(ensemble, diffusivity), first, second, onehot, pick)

    reach = 2 * (LOC_RADIUS - 1)
    tiles_reached = -(-reach // tile_rows)
    rows_of_tiles = tiles // planes
    planes_reached = min(-(-tiles_reached // rows_of_tiles), planes - 1)
    near = prior
    for d in range(1, planes_reached + 1):
        near = near + lax.ppermute(prior, "z", [(i, i + d) for i in range(planes - d)])
        near = near + lax.ppermute(prior, "z", [(i + d, i) for i in range(planes - d)])
    state = lax.all_to_all(state, mem, 0, 0, tiled=True)
    near, state = lax.optimization_barrier((near, state))
    group = mem + ("y",)
    size = lax.axis_size(group)
    spread = lax.all_to_all(
        jnp.broadcast_to(near[None], (size,) + near.shape), group, 0, 0, tiled=True
    )
    spread = spread.reshape((size // rows_of_tiles, rows_of_tiles) + near.shape)
    state = state.reshape(-1, tile_rows, width)

    out = pl.pallas_call(
        analyse,
        out_shape=shape(state.shape, f32),
        in_specs=vmem_specs(5),
        out_specs=pl.BlockSpec(memory_space=pltpu.VMEM),
        scratch_shapes=[pltpu.VMEM((state.shape[0], count), f32)],
        compiler_params=params(24),
        name="analyse",
    )(state, spread, fields, weight, cross)
    return out[:, None]


def solution(mesh):
    y = 4
    x = mesh.shape["mem"] // 2
    fine = Mesh(
        mesh.devices.reshape(x, 2, mesh.shape["space"] // y, y), ("x", "core", "z", "y")
    )
    mem, space = ("x", "core"), ("z", "y")
    placed = (P(mem, None, space, None), P(space, None), P(), P(), P(), P(), P(), P(), P())
    return jax.shard_map(
        shards, mesh=fine, in_specs=placed, out_specs=P(None, mem, space, None), check_vma=False
    )
```

```python
import jax
import jax.numpy as jnp
from jax import lax
from jax.experimental import pallas as pl
from jax.experimental.pallas import tpu as pltpu
from jax.sharding import Mesh
from jax.sharding import PartitionSpec as P

V = 4
OBS_BLOCK = 128
LOC_RADIUS = 16
ADVECT = 0.15
HALO = 2
LANES = 128
FULL = lax.Precision.HIGHEST


def vmem_specs(count):
    return [pl.BlockSpec(memory_space=pltpu.VMEM)] * count


def hbm_specs(count):
    return [pl.BlockSpec(memory_space=pltpu.HBM)] * count


def in_hbm(*arrays):
    return [pltpu.with_memory_space_constraint(a, pltpu.HBM) for a in arrays]


def fetch(pairs, sems):
    copies = [pltpu.make_async_copy(a, b, sems.at[i]) for i, (a, b) in enumerate(pairs)]
    for copy in copies:
        copy.start()
    for copy in copies:
        copy.wait()


def params(mib):
    return pltpu.CompilerParams(vmem_limit_bytes=mib * 1024 * 1024)


def prepare(tile_rows, width, place_ref, row_hbm, lon_hbm, lev_hbm, order_hbm, value_hbm, error_hbm,
            coupling_hbm, fields_ref, weight_ref, cross_ref, onehot_ref, pick_ref,
            ints, floats, coupling_ref, sems):
    count = row_hbm.shape[1]
    fetch(
        [(ref, ints.at[i]) for i, ref in enumerate((row_hbm, lon_hbm, lev_hbm, order_hbm))]
        + [(ref, floats.at[i]) for i, ref in enumerate((value_hbm, error_hbm))]
        + [(coupling_hbm, coupling_ref)],
        sems,
    )
    levels = coupling_ref.shape[0]
    tile_start = place_ref[0]
    own_level = place_ref[1]
    fields = jnp.concatenate(
        [
            ints[0].astype(jnp.float32),
            ints[1].astype(jnp.float32),
            ints[2].astype(jnp.float32),
            floats[0],
            floats[1],
            jnp.zeros((3, count), jnp.float32),
        ],
        axis=0,
    )
    source = lax.broadcasted_iota(jnp.int32, (count, count), 0)
    taken = (source == ints[3]).astype(jnp.float32)
    ordered = jnp.dot(fields, taken, precision=FULL, preferred_element_type=jnp.float32)
    fields_ref[...] = ordered
    rows = ordered[0:1]
    lons = ordered[1:2]
    levs = ordered[2:3]
    columns = jnp.concatenate([ordered, jnp.zeros((LANES - 8, count), jnp.float32)], axis=0).T
    row_col = columns[:, 0:1]
    lon_col = columns[:, 1:2]
    lev_col = columns[:, 2:3]

    def near(drow, dlon):
        dlon = jnp.minimum(dlon, width - dlon)
        close = jnp.maximum(0.0, 1.0 - (drow + dlon) / LOC_RADIUS)
        return close * close

    coupled = jnp.zeros((count, levels), jnp.float32)
    coupled_own = jnp.zeros((count, 1), jnp.float32)
    table = coupling_ref[...]
    lane = lax.broadcasted_iota(jnp.int32, (levels, levels), 1)
    own = jnp.sum(jnp.where(lane == own_level, table, 0.0), axis=1, keepdims=True)
    for level in range(levels):
        here = lev_col == level
        coupled = jnp.where(here, table[level:level + 1, :], coupled)
        coupled_own = jnp.where(here, own[level:level + 1, :], coupled_own)
    cell_lon = lax.broadcasted_iota(jnp.int32, (1, width), 1).astype(jnp.float32)
    dlon = jnp.abs(cell_lon - lon_col)
    for row in range(tile_rows):
        drow = jnp.abs((tile_start + row).astype(jnp.float32) - row_col)
        weight_ref[:, row * width:(row + 1) * width] = coupled_own * near(drow, dlon)

    first = slice(0, OBS_BLOCK)
    second = slice(OBS_BLOCK, 2 * OBS_BLOCK)
    between = jnp.zeros((OBS_BLOCK, OBS_BLOCK), jnp.float32)
    for level in range(levels):
        between = jnp.where(levs[:, second] == level, coupled[first, level:level + 1], between)
    cross_ref[...] = between * near(
        jnp.abs(row_col[first] - rows[:, second]), jnp.abs(lon_col[first] - lons[:, second])
    )

    lon_id = lax.broadcasted_iota(jnp.int32, (width, count), 0).astype(jnp.float32)
    onehot_ref[...] = (lon_id == lons).astype(jnp.bfloat16)
    heights = levels // V
    slot = lax.broadcasted_iota(jnp.int32, (8, count), 0)
    half = slot // tile_rows
    inside = rows - tile_start.astype(jnp.float32) == (slot - half * tile_rows).astype(jnp.float32)
    for height in range(heights):
        for p in range(V // 2):
            there = levs == ((2 * p + half) * heights + height).astype(jnp.float32)
            pick_ref[height * (V // 2) + p] = jnp.where(inside & there, 1.0, 0.0)


def edges(place_ref, x_hbm, diff_hbm, first_ref, second_ref, held_ref, diff_ref, sems):
    members, levels, tile_rows, width = x_hbm.shape
    extra = members * levels
    odd = place_ref[2] == 1
    copies = [pltpu.make_async_copy(diff_hbm, diff_ref, sems.at[members])]
    copies += [pltpu.make_async_copy(x_hbm.at[i], held_ref.at[i], sems.at[i]) for i in range(members)]
    for copy in copies:
        copy.start()

    def give(low_ref, high_ref):
        for member in range(members):
            part = slice(member * levels, (member + 1) * levels)
            copies[member + 1].wait()
            low_ref[part] = held_ref[member, :, :HALO, :]
            high_ref[part] = held_ref[member, :, tile_rows - HALO:, :]
        copies[0].wait()
        low_ref[extra] = diff_ref[:HALO, :]
        high_ref[extra] = diff_ref[tile_rows - HALO:, :]

    @pl.when(odd)
    def _():
        give(second_ref, first_ref)

    @pl.when(jnp.logical_not(odd))
    def _():
        give(first_ref, second_ref)


def forecast(place_ref, x_hbm, diff_hbm, first_hbm, second_hbm, onehot_ref, pick_ref, prior_ref, out_hbm,
             wide_ref, own_ref, pair_ref, diff_ref, diff_sems, in_sems, out_sems):
    members, levels, tile_rows, width = x_hbm.shape
    heights = levels // V
    deep = tile_rows + 2 * HALO
    extra = members * levels
    top, own, bottom = pl.ds(0, HALO), pl.ds(HALO, tile_rows), pl.ds(HALO + tile_rows, HALO)

    odd = place_ref[2] == 1

    def arrivals(member, low_hbm, high_hbm):
        part = pl.ds(member * levels, levels)
        return [
            pltpu.make_async_copy(x_hbm.at[member], wide_ref.at[member, :, own], in_sems.at[member, 0]),
            pltpu.make_async_copy(low_hbm.at[part], wide_ref.at[member, :, top], in_sems.at[member, 1]),
            pltpu.make_async_copy(high_hbm.at[part], wide_ref.at[member, :, bottom], in_sems.at[member, 2]),
        ]

    def departure(member):
        return pltpu.make_async_copy(own_ref.at[:, member], out_hbm.at[:, member], out_sems.at[member])

    def take(low_hbm, high_hbm):
        diffs = [
            pltpu.make_async_copy(diff_hbm, diff_ref.at[own], diff_sems.at[0]),
            pltpu.make_async_copy(low_hbm.at[extra], diff_ref.at[top], diff_sems.at[1]),
            pltpu.make_async_copy(high_hbm.at[extra], diff_ref.at[bottom], diff_sems.at[2]),
        ]
        for copy in diffs:
            copy.start()
        for member in range(members):
            for copy in arrivals(member, low_hbm, high_hbm):
                copy.start()
        for copy in diffs:
            copy.wait()

    @pl.when(odd)
    def _():
        take(second_hbm, first_hbm)

    @pl.when(jnp.logical_not(odd))
    def _():
        take(first_hbm, second_hbm)

    diff = diff_ref[...]
    keep = 1.0 - 4.0 * diff
    upper = lax.broadcasted_iota(jnp.int32, (deep, width), 0) < tile_rows

    def spread(diff, wind_u, wind_w):
        push_u, push_w = ADVECT * wind_u, ADVECT * wind_w
        return diff - push_u, diff + push_u, diff - push_w, diff + push_w

    def moved(keep, ways, q, north, south):
        from_east, from_west, from_north, from_south = ways
        return (
            keep * q
            + (from_east * pltpu.roll(q, width - 1, 1) + from_west * pltpu.roll(q, 1, 1))
            + (from_north * north + from_south * south)
        )

    def paired(a, b, shift):
        return jnp.where(
            upper,
            pltpu.roll(a, deep - HALO - shift, 0),
            pltpu.roll(b, tile_rows - HALO - shift, 0),
        )

    two_diff, two_keep = paired(diff, diff, 0), paired(keep, keep, 0)

    @pl.loop(0, members)
    def _(member):
        for copy in arrivals(member, first_hbm, second_hbm):
            copy.wait()
        for height in range(heights):
            q = [wide_ref[member, v * heights + height] for v in range(V)]
            ways = spread(diff, q[0], q[1])
            q = [moved(keep, ways, a, pltpu.roll(a, deep - 1, 0), pltpu.roll(a, 1, 0)) for a in q]
            ways = spread(two_diff, paired(q[0], q[0], 0), paired(q[1], q[1], 0))
            for p in range(V // 2):
                a, b = q[2 * p], q[2 * p + 1]
                pair = moved(two_keep, ways, paired(a, b, 0), paired(a, b, 1), paired(a, b, -1))
                pair_ref[height * (V // 2) + p, member] = pair
                own_ref[2 * p * heights + height, member] = pair[:tile_rows]
                own_ref[(2 * p + 1) * heights + height, member] = pair[tile_rows:]
        departure(member).start()

    count = onehot_ref.shape[1]
    total = jnp.zeros((members, deep, count), jnp.float32)
    for v in range(V):
        rest = pair_ref[v].reshape(members * deep, width)
        found = jnp.zeros((members * deep, count), jnp.float32)
        for _ in range(3):
            part = rest.astype(jnp.bfloat16)
            rest = rest - part.astype(jnp.float32)
            found = found + jnp.dot(part, onehot_ref[...], preferred_element_type=jnp.float32)
        total = total + found.reshape(members, deep, -1) * pick_ref[v][None]
    prior = jnp.sum(total, axis=1)
    for m in range(members):
        prior_ref[:, m * count:(m + 1) * count] = prior[m:m + 1]
    for member in range(members):
        departure(member).wait()


def split(a):
    high = a.astype(jnp.bfloat16)
    return high, (a - high.astype(jnp.float32)).astype(jnp.bfloat16)

def exactdot(a, b):
    return jnp.dot(a, b, precision=lax.Precision.HIGHEST, preferred_element_type=jnp.float32)

def adjust(prior, values, errors):
    members = prior.shape[0]
    mean = jnp.sum(prior, axis=0, keepdims=True) / members
    dev = prior - mean
    var = jnp.sum(dev * dev, axis=0, keepdims=True) / (members - 1) + 1e-06
    post_var = 1.0 / (1.0 / var + 1.0 / errors)
    post_mean = post_var * (mean / var + values / errors)
    shrink = jnp.sqrt(errors / (errors + var))
    incr = post_mean + shrink * dev - prior
    gain = dev / ((members - 1) * var)
    return incr, gain

def three(a, axis):
    high, low = split(a)
    order = [high, high, low] if axis == 1 else [high, low, high]
    return jnp.concatenate(order, axis=axis)

def thin(gain):
    high = gain.astype(jnp.bfloat16).astype(jnp.float32)
    return jnp.concatenate([high, high, gain - high], axis=0).T.astype(jnp.bfloat16)

def onedot(a, b):
    return jnp.dot(a, b, preferred_element_type=jnp.float32)

def analyse(x_ref, prior_ref, fields_ref, weight_ref, cross_ref, out_ref, scratch):
    members, tile_rows, width = x_ref.shape
    cores, tiles, chips, _, _ = prior_ref.shape
    planes = cores * chips
    count = fields_ref.shape[1]
    share = members // planes
    for i in range(planes):
        core, chip = i % cores, i // cores
        for m in range(share):
            at = slice(m * count, (m + 1) * count)
            line = prior_ref[core, 0, chip, :, at]
            for t in range(1, tiles):
                line = line + prior_ref[core, t, chip, :, at]
            scratch[i * share + m:i * share + m + 1, :] = line
    prior = scratch[...]
    values = fields_ref[3:4]
    errors = fields_ref[4:5]
    first = slice(0, OBS_BLOCK)
    second = slice(OBS_BLOCK, 2 * OBS_BLOCK)
    incr0, gain0 = adjust(prior[:, first], values[:, first], errors[:, first])
    later = prior[:, second]
    later = later + exactdot(incr0, cross_ref[...] * exactdot(gain0.T, later))
    incr1, gain1 = adjust(later, values[:, second], errors[:, second])
    incr0, incr1 = three(incr0, 1), three(incr1, 1)
    gain0, gain1 = thin(gain0), thin(gain1)
    x = jnp.concatenate([x_ref[:, row, :] for row in range(tile_rows)], axis=1)
    x = x + onedot(incr0, three(weight_ref[first, :] * onedot(gain0, three(x, 0)), 0))
    x = x + onedot(incr1, three(weight_ref[second, :] * onedot(gain1, three(x, 0)), 0))
    for row in range(tile_rows):
        out_ref[:, row, :] = x[:, row * width:(row + 1) * width]


def shards(ensemble, diffusivity, obs_row, obs_lon, obs_level, obs_order, obs_value, obs_error, coupling):
    members, levels, tile_rows, width = ensemble.shape
    count = obs_row.shape[0]
    space = ("z", "y")
    mem = ("x", "core")
    tiles = lax.axis_size(space)
    planes = lax.axis_size("z")
    own_level = lax.axis_index(mem)
    tile = lax.axis_index(space)
    place = jnp.stack([tile * tile_rows, own_level, tile % 2]).astype(jnp.int32)
    cells = tile_rows * width
    shape = jax.ShapeDtypeStruct
    f32 = jnp.float32

    extra = members * levels
    smem = [pl.BlockSpec(memory_space=pltpu.SMEM)]
    first, second = pl.pallas_call(
        edges,
        out_shape=[pltpu.VMEM((extra + 1, HALO, width), f32)] * 2,
        in_specs=smem + hbm_specs(2),
        out_specs=vmem_specs(2),
        scratch_shapes=[
            pltpu.VMEM(ensemble.shape, f32),
            pltpu.VMEM((tile_rows, width), f32),
            pltpu.SemaphoreType.DMA((members + 1,)),
        ],
        compiler_params=params(8),
        name="edges",
    )(place, *in_hbm(ensemble, diffusivity))

    def swap(message, start):
        pairs = [(i, i + 1) for i in range(start, tiles - 1, 2)]
        return lax.ppermute(message, space, pairs + [(j, i) for i, j in pairs])

    first, second = swap(first, 1), swap(second, 0)

    line = lambda a: a.reshape(1, count)
    fields, weight, cross, onehot, pick = pl.pallas_call(
        lambda *refs: prepare(tile_rows, width, *refs),
        out_shape=[
            shape((8, count), f32),
            shape((count, cells), f32),
            shape((OBS_BLOCK, OBS_BLOCK), f32),
            shape((width, count), jnp.bfloat16),
            shape((V, 8, count), f32),
        ],
        in_specs=smem + hbm_specs(7),
        out_specs=vmem_specs(5),
        scratch_shapes=[
            pltpu.VMEM((4, 1, count), jnp.int32),
            pltpu.VMEM((2, 1, count), f32),
            pltpu.VMEM((levels, levels), f32),
            pltpu.SemaphoreType.DMA((7,)),
        ],
        compiler_params=params(16),
        cost_estimate=pl.CostEstimate(flops=10_000_000, bytes_accessed=4_000_000, transcendentals=0),
        name="prepare",
    )(place, *in_hbm(line(obs_row), line(obs_lon), line(obs_level), line(obs_order), line(obs_value),
                     line(obs_error), coupling))

    deep = tile_rows + 2 * HALO
    prior, state = pl.pallas_call(
        forecast,
        out_shape=[
            shape((1, members * count), f32),
            pltpu.HBM((levels, members, tile_rows, width), f32),
        ],
        in_specs=smem + hbm_specs(4) + vmem_specs(2),
        out_specs=vmem_specs(1) + hbm_specs(1),
        scratch_shapes=[
            pltpu.VMEM((members, levels, deep, width), f32),
            pltpu.VMEM((levels, members, tile_rows, width), f32),
            pltpu.VMEM((V, members, deep, width), f32),
            pltpu.VMEM((deep, width), f32),
            pltpu.SemaphoreType.DMA((3,)),
            pltpu.SemaphoreType.DMA((members, 3)),
            pltpu.SemaphoreType.DMA((members,)),
        ],
        compiler_params=params(16),
        name="forecast",
    )(place, *in_hbm(ensemble, diffusivity), first, second, onehot, pick)

    reach = 2 * (LOC_RADIUS - 1)
    tiles_reached = -(-reach // tile_rows)
    rows_of_tiles = tiles // planes
    planes_reached = min(-(-tiles_reached // rows_of_tiles), planes - 1)
    near = prior
    for d in range(1, planes_reached + 1):
        near = near + lax.ppermute(prior, "z", [(i, i + d) for i in range(planes - d)])
        near = near + lax.ppermute(prior, "z", [(i + d, i) for i in range(planes - d)])
    state = lax.all_to_all(state, mem, 0, 0, tiled=True)
    near, state = lax.optimization_barrier((near, state))
    group = ("core", "y", "x")
    size = lax.axis_size(group)
    spread = lax.all_to_all(
        jnp.broadcast_to(near[None], (size,) + near.shape), group, 0, 0, tiled=True
    )
    spread = spread.reshape(tuple(lax.axis_size(a) for a in group) + near.shape)
    state = state.reshape(-1, tile_rows, width)

    out = pl.pallas_call(
        analyse,
        out_shape=shape(state.shape, f32),
        in_specs=vmem_specs(5),
        out_specs=pl.BlockSpec(memory_space=pltpu.VMEM),
        scratch_shapes=[pltpu.VMEM((state.shape[0], count), f32)],
        compiler_params=params(24),
        name="analyse",
    )(state, spread, fields, weight, cross)
    return out[:, None]


def solution(mesh):
    y = 4
    x = mesh.shape["mem"] // 2
    fine = Mesh(
        mesh.devices.reshape(x, 2, mesh.shape["space"] // y, y), ("x", "core", "z", "y")
    )
    mem, space = ("x", "core"), ("z", "y")
    placed = (P(mem, None, space, None), P(space, None), P(), P(), P(), P(), P(), P(), P())
    return jax.shard_map(
        shards, mesh=fine, in_specs=placed, out_specs=P(None, mem, space, None), check_vma=False
    )
```

```python
import jax
import jax.numpy as jnp
from jax import lax
from jax.experimental import pallas as pl
from jax.experimental.pallas import tpu as pltpu
from jax.sharding import Mesh
from jax.sharding import PartitionSpec as P

V = 4
OBS_BLOCK = 128
LOC_RADIUS = 16
ADVECT = 0.15
HALO = 2
LANES = 128
FULL = lax.Precision.HIGHEST


def vmem_specs(count):
    return [pl.BlockSpec(memory_space=pltpu.VMEM)] * count


def hbm_specs(count):
    return [pl.BlockSpec(memory_space=pltpu.HBM)] * count


def in_hbm(*arrays):
    return [pltpu.with_memory_space_constraint(a, pltpu.HBM) for a in arrays]


def fetch(pairs, sems):
    copies = [pltpu.make_async_copy(a, b, sems.at[i]) for i, (a, b) in enumerate(pairs)]
    for copy in copies:
        copy.start()
    for copy in copies:
        copy.wait()


def params(mib):
    return pltpu.CompilerParams(vmem_limit_bytes=mib * 1024 * 1024)


def prepare(tile_rows, width, place_ref, row_hbm, lon_hbm, lev_hbm, order_hbm, value_hbm, error_hbm,
            coupling_hbm, fields_ref, weight_ref, cross_ref, onehot_ref, pick_ref,
            ints, floats, coupling_ref, sems):
    count = row_hbm.shape[1]
    fetch(
        [(ref, ints.at[i]) for i, ref in enumerate((row_hbm, lon_hbm, lev_hbm, order_hbm))]
        + [(ref, floats.at[i]) for i, ref in enumerate((value_hbm, error_hbm))]
        + [(coupling_hbm, coupling_ref)],
        sems,
    )
    levels = coupling_ref.shape[0]
    tile_start = place_ref[0]
    own_level = place_ref[1]
    fields = jnp.concatenate(
        [
            ints[0].astype(jnp.float32),
            ints[1].astype(jnp.float32),
            ints[2].astype(jnp.float32),
            floats[0],
            floats[1],
            jnp.zeros((3, count), jnp.float32),
        ],
        axis=0,
    )
    source = lax.broadcasted_iota(jnp.int32, (count, count), 0)
    taken = (source == ints[3]).astype(jnp.float32)
    ordered = jnp.dot(fields, taken, precision=FULL, preferred_element_type=jnp.float32)
    fields_ref[...] = ordered
    rows = ordered[0:1]
    lons = ordered[1:2]
    levs = ordered[2:3]
    columns = jnp.concatenate([ordered, jnp.zeros((LANES - 8, count), jnp.float32)], axis=0).T
    row_col = columns[:, 0:1]
    lon_col = columns[:, 1:2]
    lev_col = columns[:, 2:3]

    def near(drow, dlon):
        dlon = jnp.minimum(dlon, width - dlon)
        close = jnp.maximum(0.0, 1.0 - (drow + dlon) / LOC_RADIUS)
        return close * close

    coupled = jnp.zeros((count, levels), jnp.float32)
    coupled_own = jnp.zeros((count, 1), jnp.float32)
    table = coupling_ref[...]
    lane = lax.broadcasted_iota(jnp.int32, (levels, levels), 1)
    own = jnp.sum(jnp.where(lane == own_level, table, 0.0), axis=1, keepdims=True)
    for level in range(levels):
        here = lev_col == level
        coupled = jnp.where(here, table[level:level + 1, :], coupled)
        coupled_own = jnp.where(here, own[level:level + 1, :], coupled_own)
    cell_lon = lax.broadcasted_iota(jnp.int32, (1, width), 1).astype(jnp.float32)
    dlon = jnp.abs(cell_lon - lon_col)
    for row in range(tile_rows):
        drow = jnp.abs((tile_start + row).astype(jnp.float32) - row_col)
        weight_ref[:, row * width:(row + 1) * width] = coupled_own * near(drow, dlon)

    first = slice(0, OBS_BLOCK)
    second = slice(OBS_BLOCK, 2 * OBS_BLOCK)
    between = jnp.zeros((OBS_BLOCK, OBS_BLOCK), jnp.float32)
    for level in range(levels):
        between = jnp.where(levs[:, second] == level, coupled[first, level:level + 1], between)
    cross_ref[...] = between * near(
        jnp.abs(row_col[first] - rows[:, second]), jnp.abs(lon_col[first] - lons[:, second])
    )

    lon_id = lax.broadcasted_iota(jnp.int32, (width, count), 0).astype(jnp.float32)
    onehot_ref[...] = (lon_id == lons).astype(jnp.bfloat16)
    heights = levels // V
    slot = lax.broadcasted_iota(jnp.int32, (8, count), 0)
    half = slot // tile_rows
    inside = rows - tile_start.astype(jnp.float32) == (slot - half * tile_rows).astype(jnp.float32)
    for height in range(heights):
        for p in range(V // 2):
            there = levs == ((2 * p + half) * heights + height).astype(jnp.float32)
            pick_ref[height * (V // 2) + p] = jnp.where(inside & there, 1.0, 0.0)


def edges(place_ref, x_hbm, diff_hbm, first_ref, second_ref, held_ref, diff_ref, sems):
    members, levels, tile_rows, width = x_hbm.shape
    extra = members * levels
    odd = place_ref[2] == 1
    copies = [pltpu.make_async_copy(diff_hbm, diff_ref, sems.at[members])]
    copies += [pltpu.make_async_copy(x_hbm.at[i], held_ref.at[i], sems.at[i]) for i in range(members)]
    for copy in copies:
        copy.start()

    def give(low_ref, high_ref):
        for member in range(members):
            part = slice(member * levels, (member + 1) * levels)
            copies[member + 1].wait()
            low_ref[part] = held_ref[member, :, :HALO, :]
            high_ref[part] = held_ref[member, :, tile_rows - HALO:, :]
        copies[0].wait()
        low_ref[extra] = diff_ref[:HALO, :]
        high_ref[extra] = diff_ref[tile_rows - HALO:, :]

    @pl.when(odd)
    def _():
        give(second_ref, first_ref)

    @pl.when(jnp.logical_not(odd))
    def _():
        give(first_ref, second_ref)


def forecast(place_ref, x_hbm, diff_hbm, first_hbm, second_hbm, pair_ref, out_hbm,
             wide_ref, own_ref, diff_ref, diff_sems, in_sems, out_sems):
    members, levels, tile_rows, width = x_hbm.shape
    heights = levels // V
    deep = tile_rows + 2 * HALO
    extra = members * levels
    top, own, bottom = pl.ds(0, HALO), pl.ds(HALO, tile_rows), pl.ds(HALO + tile_rows, HALO)

    odd = place_ref[2] == 1

    def arrivals(member, low_hbm, high_hbm):
        part = pl.ds(member * levels, levels)
        return [
            pltpu.make_async_copy(x_hbm.at[member], wide_ref.at[member, :, own], in_sems.at[member, 0]),
            pltpu.make_async_copy(low_hbm.at[part], wide_ref.at[member, :, top], in_sems.at[member, 1]),
            pltpu.make_async_copy(high_hbm.at[part], wide_ref.at[member, :, bottom], in_sems.at[member, 2]),
        ]

    def departure(member):
        return pltpu.make_async_copy(own_ref.at[:, member], out_hbm.at[:, member], out_sems.at[member])

    def take(low_hbm, high_hbm):
        diffs = [
            pltpu.make_async_copy(diff_hbm, diff_ref.at[own], diff_sems.at[0]),
            pltpu.make_async_copy(low_hbm.at[extra], diff_ref.at[top], diff_sems.at[1]),
            pltpu.make_async_copy(high_hbm.at[extra], diff_ref.at[bottom], diff_sems.at[2]),
        ]
        for copy in diffs:
            copy.start()
        for member in range(members):
            for copy in arrivals(member, low_hbm, high_hbm):
                copy.start()
        for copy in diffs:
            copy.wait()

    @pl.when(odd)
    def _():
        take(second_hbm, first_hbm)

    @pl.when(jnp.logical_not(odd))
    def _():
        take(first_hbm, second_hbm)

    diff = diff_ref[...]
    keep = 1.0 - 4.0 * diff
    upper = lax.broadcasted_iota(jnp.int32, (deep, width), 0) < tile_rows

    def spread(diff, wind_u, wind_w):
        push_u, push_w = ADVECT * wind_u, ADVECT * wind_w
        return diff - push_u, diff + push_u, diff - push_w, diff + push_w

    def moved(keep, ways, q, north, south):
        from_east, from_west, from_north, from_south = ways
        return (
            keep * q
            + (from_east * pltpu.roll(q, width - 1, 1) + from_west * pltpu.roll(q, 1, 1))
            + (from_north * north + from_south * south)
        )

    def paired(a, b, shift):
        return jnp.where(
            upper,
            pltpu.roll(a, deep - HALO - shift, 0),
            pltpu.roll(b, tile_rows - HALO - shift, 0),
        )

    two_diff, two_keep = paired(diff, diff, 0), paired(keep, keep, 0)

    @pl.loop(0, members)
    def _(member):
        for copy in arrivals(member, first_hbm, second_hbm):
            copy.wait()
        for height in range(heights):
            q = [wide_ref[member, v * heights + height] for v in range(V)]
            ways = spread(diff, q[0], q[1])
            q = [moved(keep, ways, a, pltpu.roll(a, deep - 1, 0), pltpu.roll(a, 1, 0)) for a in q]
            ways = spread(two_diff, paired(q[0], q[0], 0), paired(q[1], q[1], 0))
            for p in range(V // 2):
                a, b = q[2 * p], q[2 * p + 1]
                pair = moved(two_keep, ways, paired(a, b, 0), paired(a, b, 1), paired(a, b, -1))
                pair_ref[height * (V // 2) + p, member] = pair
                own_ref[2 * p * heights + height, member] = pair[:tile_rows]
                own_ref[(2 * p + 1) * heights + height, member] = pair[tile_rows:]
        departure(member).start()

    for member in range(members):
        departure(member).wait()


def gather(pair_ref, onehot_ref, pick_ref, prior_ref):
    _, members, deep, width = pair_ref.shape
    count = onehot_ref.shape[1]
    total = jnp.zeros((members, deep, count), jnp.float32)
    for v in range(V):
        rest = pair_ref[v].reshape(members * deep, width)
        found = jnp.zeros((members * deep, count), jnp.float32)
        for _ in range(3):
            part = rest.astype(jnp.bfloat16)
            rest = rest - part.astype(jnp.float32)
            found = found + jnp.dot(part, onehot_ref[...], preferred_element_type=jnp.float32)
        total = total + found.reshape(members, deep, -1) * pick_ref[v][None]
    prior = jnp.sum(total, axis=1)
    for m in range(members):
        prior_ref[:, m * count:(m + 1) * count] = prior[m:m + 1]


def split(a):
    high = a.astype(jnp.bfloat16)
    return high, (a - high.astype(jnp.float32)).astype(jnp.bfloat16)

def exactdot(a, b):
    return jnp.dot(a, b, precision=lax.Precision.HIGHEST, preferred_element_type=jnp.float32)

def adjust(prior, values, errors):
    members = prior.shape[0]
    mean = jnp.sum(prior, axis=0, keepdims=True) / members
    dev = prior - mean
    var = jnp.sum(dev * dev, axis=0, keepdims=True) / (members - 1) + 1e-06
    post_var = 1.0 / (1.0 / var + 1.0 / errors)
    post_mean = post_var * (mean / var + values / errors)
    shrink = jnp.sqrt(errors / (errors + var))
    incr = post_mean + shrink * dev - prior
    gain = dev / ((members - 1) * var)
    return incr, gain

def three(a, axis):
    high, low = split(a)
    order = [high, high, low] if axis == 1 else [high, low, high]
    return jnp.concatenate(order, axis=axis)

def thin(gain):
    high = gain.astype(jnp.bfloat16).astype(jnp.float32)
    return jnp.concatenate([high, high, gain - high], axis=0).T.astype(jnp.bfloat16)

def onedot(a, b):
    return jnp.dot(a, b, preferred_element_type=jnp.float32)

def analyse(x_ref, prior_ref, fields_ref, weight_ref, cross_ref, out_ref, scratch):
    members, tile_rows, width = x_ref.shape
    cores, tiles, chips, _, _ = prior_ref.shape
    planes = cores * chips
    count = fields_ref.shape[1]
    share = members // planes
    for i in range(planes):
        core, chip = i % cores, i // cores
        for m in range(share):
            at = slice(m * count, (m + 1) * count)
            line = prior_ref[core, 0, chip, :, at]
            for t in range(1, tiles):
                line = line + prior_ref[core, t, chip, :, at]
            scratch[i * share + m:i * share + m + 1, :] = line
    prior = scratch[...]
    values = fields_ref[3:4]
    errors = fields_ref[4:5]
    first = slice(0, OBS_BLOCK)
    second = slice(OBS_BLOCK, 2 * OBS_BLOCK)
    incr0, gain0 = adjust(prior[:, first], values[:, first], errors[:, first])
    later = prior[:, second]
    later = later + exactdot(incr0, cross_ref[...] * exactdot(gain0.T, later))
    incr1, gain1 = adjust(later, values[:, second], errors[:, second])
    incr0, incr1 = three(incr0, 1), three(incr1, 1)
    gain0, gain1 = thin(gain0), thin(gain1)
    x = jnp.concatenate([x_ref[:, row, :] for row in range(tile_rows)], axis=1)
    x = x + onedot(incr0, three(weight_ref[first, :] * onedot(gain0, three(x, 0)), 0))
    x = x + onedot(incr1, three(weight_ref[second, :] * onedot(gain1, three(x, 0)), 0))
    for row in range(tile_rows):
        out_ref[:, row, :] = x[:, row * width:(row + 1) * width]


def shards(ensemble, diffusivity, obs_row, obs_lon, obs_level, obs_order, obs_value, obs_error, coupling):
    members, levels, tile_rows, width = ensemble.shape
    count = obs_row.shape[0]
    space = ("z", "y")
    mem = ("x", "core")
    tiles = lax.axis_size(space)
    planes = lax.axis_size("z")
    own_level = lax.axis_index(mem)
    tile = lax.axis_index(space)
    place = jnp.stack([tile * tile_rows, own_level, tile % 2]).astype(jnp.int32)
    cells = tile_rows * width
    shape = jax.ShapeDtypeStruct
    f32 = jnp.float32

    extra = members * levels
    smem = [pl.BlockSpec(memory_space=pltpu.SMEM)]
    first, second = pl.pallas_call(
        edges,
        out_shape=[pltpu.VMEM((extra + 1, HALO, width), f32)] * 2,
        in_specs=smem + hbm_specs(2),
        out_specs=vmem_specs(2),
        scratch_shapes=[
            pltpu.VMEM(ensemble.shape, f32),
            pltpu.VMEM((tile_rows, width), f32),
            pltpu.SemaphoreType.DMA((members + 1,)),
        ],
        compiler_params=params(8),
        name="edges",
    )(place, *in_hbm(ensemble, diffusivity))

    def swap(message, start):
        pairs = [(i, i + 1) for i in range(start, tiles - 1, 2)]
        return lax.ppermute(message, space, pairs + [(j, i) for i, j in pairs])

    first, second = swap(first, 1), swap(second, 0)

    line = lambda a: a.reshape(1, count)
    fields, weight, cross, onehot, pick = pl.pallas_call(
        lambda *refs: prepare(tile_rows, width, *refs),
        out_shape=[
            shape((8, count), f32),
            shape((count, cells), f32),
            shape((OBS_BLOCK, OBS_BLOCK), f32),
            shape((width, count), jnp.bfloat16),
            shape((V, 8, count), f32),
        ],
        in_specs=smem + hbm_specs(7),
        out_specs=vmem_specs(5),
        scratch_shapes=[
            pltpu.VMEM((4, 1, count), jnp.int32),
            pltpu.VMEM((2, 1, count), f32),
            pltpu.VMEM((levels, levels), f32),
            pltpu.SemaphoreType.DMA((7,)),
        ],
        compiler_params=params(16),
        cost_estimate=pl.CostEstimate(flops=10_000_000, bytes_accessed=4_000_000, transcendentals=0),
        name="prepare",
    )(place, *in_hbm(line(obs_row), line(obs_lon), line(obs_level), line(obs_order), line(obs_value),
                     line(obs_error), coupling))

    deep = tile_rows + 2 * HALO
    pairs, state = pl.pallas_call(
        forecast,
        out_shape=[
            pltpu.VMEM((V, members, deep, width), f32),
            pltpu.HBM((levels, members, tile_rows, width), f32),
        ],
        in_specs=smem + hbm_specs(4),
        out_specs=vmem_specs(1) + hbm_specs(1),
        scratch_shapes=[
            pltpu.VMEM((members, levels, deep, width), f32),
            pltpu.VMEM((levels, members, tile_rows, width), f32),
            pltpu.VMEM((deep, width), f32),
            pltpu.SemaphoreType.DMA((3,)),
            pltpu.SemaphoreType.DMA((members, 3)),
            pltpu.SemaphoreType.DMA((members,)),
        ],
        compiler_params=params(16),
        name="forecast",
    )(place, *in_hbm(ensemble, diffusivity), first, second)
    prior = pl.pallas_call(
        gather,
        out_shape=shape((1, members * count), f32),
        in_specs=vmem_specs(3),
        out_specs=pl.BlockSpec(memory_space=pltpu.VMEM),
        compiler_params=params(8),
        cost_estimate=pl.CostEstimate(flops=20_000_000_000, bytes_accessed=60_000_000, transcendentals=0),
        name="gather",
    )(pairs, onehot, pick)

    reach = 2 * (LOC_RADIUS - 1)
    tiles_reached = -(-reach // tile_rows)
    rows_of_tiles = tiles // planes
    planes_reached = min(-(-tiles_reached // rows_of_tiles), planes - 1)
    core = lax.axis_index("core")
    both = lax.all_gather(prior, "core", axis=0, tiled=True).reshape(1, -1)
    near = jnp.where(core == 0, both, 0.0)
    for d in range(1, planes_reached + 1):
        ways = [(i, i + d) for i in range(planes - d)]
        ways += [(planes + i + d, planes + i) for i in range(planes - d)]
        near = near + lax.ppermute(both, ("core", "z"), ways)
    state = lax.all_to_all(state, mem, 0, 0, tiled=True)
    near, state = lax.optimization_barrier((near, state))
    near = lax.all_gather(near, "core", axis=0, tiled=True)
    near = (near[0:1] + near[1:2]).reshape(2, -1)
    near = jnp.where(core == 0, near[0:1], near[1:2])
    group = ("core", "y", "x")
    size = lax.axis_size(group)
    spread = lax.all_to_all(
        jnp.broadcast_to(near[None], (size,) + near.shape), group, 0, 0, tiled=True
    )
    spread = spread.reshape(tuple(lax.axis_size(a) for a in group) + near.shape)
    state = state.reshape(-1, tile_rows, width)

    out = pl.pallas_call(
        analyse,
        out_shape=shape(state.shape, f32),
        in_specs=vmem_specs(5),
        out_specs=pl.BlockSpec(memory_space=pltpu.VMEM),
        scratch_shapes=[pltpu.VMEM((state.shape[0], count), f32)],
        compiler_params=params(24),
        name="analyse",
    )(state, spread, fields, weight, cross)
    return out[:, None]


def solution(mesh):
    y = 4
    x = mesh.shape["mem"] // 2
    fine = Mesh(
        mesh.devices.reshape(x, 2, mesh.shape["space"] // y, y), ("x", "core", "z", "y")
    )
    mem, space = ("x", "core"), ("z", "y")
    placed = (P(mem, None, space, None), P(space, None), P(), P(), P(), P(), P(), P(), P())
    return jax.shard_map(
        shards, mesh=fine, in_specs=placed, out_specs=P(None, mem, space, None), check_vma=False
    )
```
